32 devices in a mesh: groups: 2 (over x), ctx: 16 (over z, y, core).
Axes of the slice: x: 2, y: 2, z: 4, core: 2. Of those that a mesh axis runs over, the one named last changes fastest.
Arguments:
- queries: bfloat16 [16384, 2048], P(('groups', 'ctx')), parts along dimension 0, may hold values from -400 to 400
- keys: bfloat16 [16384, 512], P(('groups', 'ctx')), parts along dimension 0, may hold values from -8 to 8
- values: bfloat16 [16384, 512], P(('groups', 'ctx')), parts along dimension 0, may hold values from -6 to 6
- grad_out: bfloat16 [16384, 2048], P(('groups', 'ctx')), parts along dimension 0, may hold values from -6 to 6
- seg_starts: int32 [32], P('groups'), parts along dimension 0, may hold values from 0 to 8191, as said below
- channels: int32 [16384], P(('groups', 'ctx')), parts along dimension 0, may hold values from 0 to 1
Outputs:
- grad_queries: bfloat16 [16384, 2048], P(('groups', 'ctx')), parts along dimension 0
- grad_keys: bfloat16 [16384, 512], P(('groups', 'ctx')), parts along dimension 0
- grad_values: bfloat16 [16384, 512], P(('groups', 'ctx')), parts along dimension 0
The draws below stay inside these ranges and needn't reach their ends.
There are 2 independent parts, one for each index of `groups`. The reference program is written for one: setup_inputs(seed, part) draws one part's arguments, and reference() takes and returns one part's arrays. A program takes and returns all parts, laid end to end along the dimension named above; each array names one. Nothing has to cross between parts.
Inputs may be any that keep to these rules, and one draw needn't show every extreme that they name: seg_starts[0] is 0 and the entries rise strictly; segment s runs from seg_starts[s] to the next start or the stream's end.
All inputs are finite; a program needn't handle non-finite values.
Results may differ from the reference program's by a relative error of at most 0.0055.
Values may be sent and summed in bfloat16 or wider, within the bound.
A program may use at most 128 MiB of HBM per device.

```python
import jax
import jax.numpy as jnp
from jax import lax

HQ = 16
HK = 4
HD = 128
LAG = 16
TOK_DEV = 512
SEQ = 8192
NSEG = 16


def pair_draw(key):
    key_part = jax.random.normal(jax.random.fold_in(key, 11), (SEQ, HK * HD), jnp.float32)
    key_part = jnp.clip(key_part, -8.0, 8.0)
    query_part = jax.random.normal(jax.random.fold_in(key, 12), (SEQ, HQ * HD), jnp.float32)
    return (query_part, key_part)


def draw_queries(key, part):
    return pair_draw(key)[0].astype(jnp.bfloat16)


def draw_keys(key, part):
    return pair_draw(key)[1].astype(jnp.bfloat16)


def draw_seg_starts(key, part):
    later = jax.random.permutation(jax.random.fold_in(key, 21), SEQ - 1)[:NSEG - 1] + 1
    later = jnp.sort(later.astype(jnp.int32))
    return jnp.concatenate([jnp.zeros((1,), jnp.int32), later]).astype(jnp.int32)


def set_ends(drawn, key, smallest, top_value):
    shape = drawn.shape
    place = [jax.random.randint(jax.random.fold_in(key, axis), (), 0, shape[axis]) for axis in range(len(shape))]
    drawn = drawn.at[tuple(place)].set(smallest)
    longest = shape.index(max(shape))
    place[longest] = (place[longest] + 1) % shape[longest]
    return drawn.at[tuple(place)].set(top_value)


def levels(own_key, shape, cuts, least, top_value):
    def one(axis_at, shards_of):
        heights = jax.random.uniform(jax.random.fold_in(jax.random.fold_in(own_key, 6), axis_at), (shards_of,), jnp.float32, least / len(cuts), top_value / len(cuts))
        return jnp.repeat(jnp.exp(heights), shape[axis_at] // shards_of).reshape((-1,) + (1,) * (len(shape) - axis_at - 1))

    factor_of = one(*cuts[0])
    for cut in cuts[1:]:
        factor_of = factor_of * one(*cut)
    return factor_of


def bell_draw(key, extent, spread, limit, pieces=(), held_as=jnp.bfloat16):
    gain = levels(key, extent, pieces, -0.22, 0.18) if pieces else 1.0
    result = jax.random.normal(key, extent, jnp.float32) * spread * gain
    return jnp.minimum(jnp.maximum(result, -limit), limit).astype(held_as)


def setup_inputs(seed: int = 0, part: int = 0) -> dict:
    seeds = jax.random.split(jax.random.key(seed), 7)
    part_keys = jax.random.split(jax.random.fold_in(seeds[6], part), 7)
    queries = draw_queries(jax.random.fold_in(jax.random.fold_in(seeds[6], part), 71), part)
    keys = draw_keys(jax.random.fold_in(jax.random.fold_in(seeds[6], part), 71), part)
    values = bell_draw(part_keys[2], (SEQ, HK * HD), 1.0, 6.0, ((0, 16),))
    grad_out = bell_draw(part_keys[3], (SEQ, HQ * HD), 1.0, 6.0, ((0, 16),))
    seg_starts = draw_seg_starts(jax.random.fold_in(jax.random.fold_in(seeds[6], part), 71), part)
    channels = set_ends(jax.random.randint(part_keys[5], (SEQ,), 0, 2), jax.random.fold_in(part_keys[5], 1), 0, 1).astype(jnp.int32)
    return dict(queries=queries, keys=keys, values=values, grad_out=grad_out, seg_starts=seg_starts, channels=channels)


def reference(queries, keys, values, grad_out, seg_starts, channels):
    block_rows = TOK_DEV
    blocks = SEQ // block_rows
    group_size = HQ // HK
    score_scale = HD ** -0.5
    positions = jnp.arange(SEQ, dtype=jnp.int32)
    segment = jnp.sum((seg_starts[None, :] <= positions[:, None]).astype(jnp.int32), axis=1) - 1
    pad_keys = jnp.concatenate([jnp.zeros((block_rows, HK * HD), keys.dtype), keys], axis=0)
    pad_values = jnp.concatenate([jnp.zeros((block_rows, HK * HD), values.dtype), values], axis=0)
    pad_chan = jnp.concatenate([jnp.zeros((block_rows,), jnp.int32), channels.astype(jnp.int32)], axis=0)
    pad_seg = jnp.concatenate([jnp.full((block_rows,), -1, jnp.int32), segment], axis=0)

    def one_block(block):
        first_row = (block * block_rows).astype(jnp.int32)
        query_block = lax.dynamic_slice_in_dim(queries, first_row, block_rows, 0).reshape(block_rows, HK, group_size, HD).astype(jnp.float32)
        grad_block = lax.dynamic_slice_in_dim(grad_out, first_row, block_rows, 0).reshape(block_rows, HK, group_size, HD).astype(jnp.float32)
        key_window = lax.dynamic_slice_in_dim(pad_keys, first_row, 2 * block_rows, 0).reshape(2 * block_rows, HK, HD).astype(jnp.float32)
        value_window = lax.dynamic_slice_in_dim(pad_values, first_row, 2 * block_rows, 0).reshape(2 * block_rows, HK, HD).astype(jnp.float32)
        query_pos = first_row + jnp.arange(block_rows, dtype=jnp.int32)
        key_pos = first_row - block_rows + jnp.arange(2 * block_rows, dtype=jnp.int32)
        query_seg = lax.dynamic_slice_in_dim(segment, first_row, block_rows, 0)
        key_seg = lax.dynamic_slice_in_dim(pad_seg, first_row, 2 * block_rows, 0)
        query_chan = lax.dynamic_slice_in_dim(channels.astype(jnp.int32), first_row, block_rows, 0)
        key_chan = lax.dynamic_slice_in_dim(pad_chan, first_row, 2 * block_rows, 0)
        later = query_pos[:, None]
        earlier = key_pos[None, :]
        visible = (earlier <= later) & (earlier > later - block_rows) & (earlier >= 0)
        visible = visible & (query_seg[:, None] == key_seg[None, :])
        visible = visible & ((query_chan[:, None] == key_chan[None, :]) | (earlier <= later - LAG))
        scores = jnp.einsum('ihgd,jhd->hgij', query_block, key_window) * score_scale
        row_max = jnp.max(jnp.where(visible, scores, -1e30), axis=-1)
        weights = jnp.where(visible, jnp.exp(scores - row_max[..., None]), 0.0)
        row_sum = jnp.sum(weights, axis=-1)
        probs = weights / row_sum[..., None]
        dprobs = jnp.einsum('ihgd,jhd->hgij', grad_block, value_window)
        delta = jnp.sum(probs * dprobs, axis=-1)
        dscores = lax.optimization_barrier((probs * (dprobs - delta[..., None])).astype(jnp.bfloat16)).astype(jnp.float32)
        probs_low = lax.optimization_barrier(probs.astype(jnp.bfloat16)).astype(jnp.float32)
        grad_query = jnp.einsum('hgij,jhd->ihgd', dscores, key_window) * score_scale
        grad_key = jnp.einsum('hgij,ihgd->jhd', dscores, query_block) * score_scale
        grad_value = jnp.einsum('hgij,ihgd->jhd', probs_low, grad_block)
        return grad_query.reshape(block_rows, HQ * HD).astype(jnp.bfloat16), grad_key, grad_value

    grad_query_all, grad_key_all, grad_value_all = lax.map(one_block, jnp.arange(blocks, dtype=jnp.int32))
    tail_zeros = jnp.zeros((1, block_rows, HK, HD), jnp.float32)
    grad_keys = grad_key_all[:, block_rows:] + jnp.concatenate([grad_key_all[1:, :block_rows], tail_zeros], axis=0)
    grad_values = grad_value_all[:, block_rows:] + jnp.concatenate([grad_value_all[1:, :block_rows], tail_zeros], axis=0)
    return (grad_query_all.reshape(SEQ, HQ * HD),
            grad_keys.reshape(SEQ, HK * HD).astype(jnp.bfloat16),
            grad_values.reshape(SEQ, HK * HD).astype(jnp.bfloat16))
```

```python
import functools

import jax
import jax.numpy as jnp
import numpy as np
from jax import lax
from jax.experimental import pallas as pl
from jax.experimental.pallas import tpu as pltpu
from jax.sharding import PartitionSpec as P

HQ = 16
HK = 4
HD = 128
LAG = 16
GROUP = HQ // HK
BLK = 128
MASKED = -1e30
SCALE = HD ** (-0.5)
EXP2_SCALE = float(SCALE * np.log2(np.e))

TRANS_B = (((1,), (1,)), ((), ()))
TRANS_A = (((0,), (0,)), ((), ()))


def kernel(
    count,
    seg_ref,
    chan_ref,
    q_hbm,
    k_hbm,
    v_hbm,
    g_hbm,
    gq_ref,
    gk_ref,
    gv_ref,
    q_ref,
    g_ref,
    kw_ref,
    vw_ref,
    chan_prev,
    bias_ref,
    dk_ref,
    dv_ref,
    back_send,
    back_recv,
    local_sem,
    fwd_send_sem,
    fwd_recv_sem,
    chan_sem,
    back_send_sem,
    back_recv_sem,
):
    rows = q_ref.shape[0]
    blocks = rows // BLK
    span = rows + BLK
    me = lax.axis_index("ctx")
    has_prev = me > 0
    has_next = me < count - 1

    def lanes(h, width):
        return pl.ds(pl.multiple_of(h * width, width), width)

    def local_copies(h):
        own = pl.ds(rows, rows)
        return (
            pltpu.make_async_copy(
                k_hbm.at[:, lanes(h, HD)], kw_ref.at[own, lanes(h, HD)], local_sem.at[0, h]
            ),
            pltpu.make_async_copy(
                v_hbm.at[:, lanes(h, HD)], vw_ref.at[own, lanes(h, HD)], local_sem.at[1, h]
            ),
            pltpu.make_async_copy(
                q_hbm.at[:, lanes(h, GROUP * HD)], q_ref.at[:, lanes(h, GROUP * HD)], local_sem.at[2, h]
            ),
            pltpu.make_async_copy(
                g_hbm.at[:, lanes(h, GROUP * HD)], g_ref.at[:, lanes(h, GROUP * HD)], local_sem.at[3, h]
            ),
        )

    def forward_copies(h):
        before = pl.ds(0, rows)
        return tuple(
            pltpu.make_async_remote_copy(
                src_ref=source.at[:, lanes(h, HD)],
                dst_ref=window.at[before, lanes(h, HD)],
                send_sem=fwd_send_sem.at[which, h],
                recv_sem=fwd_recv_sem.at[which, h],
                device_id={"ctx": me + 1},
                device_id_type=pl.DeviceIdType.MESH,
            )
            for which, (source, window) in enumerate(((k_hbm, kw_ref), (v_hbm, vw_ref)))
        )

    chan_copy = pltpu.make_async_remote_copy(
        src_ref=chan_ref,
        dst_ref=chan_prev,
        send_sem=chan_sem.at[0],
        recv_sem=chan_sem.at[1],
        device_id={"ctx": me + 1},
        device_id_type=pl.DeviceIdType.MESH,
    )

    def back_copy(h):
        return pltpu.make_async_remote_copy(
            src_ref=back_send.at[h],
            dst_ref=back_recv.at[h],
            send_sem=back_send_sem.at[h],
            recv_sem=back_recv_sem.at[h],
            device_id={"ctx": me - 1},
            device_id_type=pl.DeviceIdType.MESH,
        )

    barrier = pltpu.get_barrier_semaphore()

    @pl.when(has_prev)
    def _():
        pl.semaphore_signal(
            barrier, inc=1, device_id={"ctx": me - 1}, device_id_type=pl.DeviceIdType.MESH
        )

    @pl.when(has_next)
    def _():
        pl.semaphore_signal(
            barrier, inc=1, device_id={"ctx": me + 1}, device_id_type=pl.DeviceIdType.MESH
        )

    for h in range(HK):
        for copy in local_copies(h):
            copy.start()
    pl.semaphore_wait(barrier, has_prev.astype(jnp.int32) + has_next.astype(jnp.int32))

    @pl.when(has_next)
    def _():
        chan_copy.start()
        for h in range(HK):
            for copy in forward_copies(h):
                copy.start()

    @pl.when(jnp.logical_not(has_prev))
    def _():
        kw_ref[0:rows, :] = jnp.zeros((rows, HK * HD), jnp.bfloat16)
        vw_ref[0:rows, :] = jnp.zeros((rows, HK * HD), jnp.bfloat16)
        chan_prev[...] = jnp.zeros_like(chan_prev)

    @pl.when(has_prev)
    def _():
        chan_copy.wait_recv()

    def column(row):
        return jnp.transpose(jnp.broadcast_to(row, (BLK, BLK)))

    first_row = me * rows
    for b in range(blocks):
        here = slice(b * BLK, (b + 1) * BLK)
        position = first_row + b * BLK + lax.broadcasted_iota(jnp.int32, (1, BLK), 1)
        start = jnp.zeros((1, BLK), jnp.int32)
        for s in range(seg_ref.shape[0]):
            start = jnp.maximum(start, jnp.where(seg_ref[s] <= position, seg_ref[s], 0))
        start = start - (first_row - rows + b * BLK)
        query_chan = chan_ref[:, here]
        query = lax.broadcasted_iota(jnp.int32, (BLK, BLK), 1)
        for c in range(span // BLK):
            key = c * BLK + lax.broadcasted_iota(jnp.int32, (BLK, BLK), 0)
            place = (b + c) * BLK
            if place < rows:
                key_chan = chan_prev[:, place : place + BLK]
            else:
                key_chan = chan_ref[:, place - rows : place - rows + BLK]
            allowed = (key > query) & (key <= query + rows) & (key >= start)
            allowed = allowed & (
                (column(key_chan) == query_chan) | (key <= query + (rows - LAG))
            )
            bias_ref[b, c * BLK : (c + 1) * BLK, :] = jnp.where(allowed, 0.0, MASKED)

    def head_step(h, carry):
        for copy in local_copies(h):
            copy.wait()

        @pl.when(has_prev)
        def _():
            for copy in forward_copies(h):
                copy.wait_recv()

        for b in range(blocks):
            here = slice(b * BLK, (b + 1) * BLK)
            window = slice(b * BLK, b * BLK + span)
            key = kw_ref[window, lanes(h, HD)]
            value = vw_ref[window, lanes(h, HD)]
            bias = bias_ref[b]
            bias = jnp.concatenate([bias, bias], axis=1)
            grad_key = None
            grad_value = None
            for pair in range(GROUP // 2):
                heads = [h * GROUP + 2 * pair, h * GROUP + 2 * pair + 1]
                query = jnp.concatenate([q_ref[here, lanes(i, HD)] for i in heads], axis=0)
                grad = jnp.concatenate([g_ref[here, lanes(i, HD)] for i in heads], axis=0)
                scores = (
                    lax.dot_general(key, query, TRANS_B, preferred_element_type=jnp.float32) + bias
                )
                top = jnp.max(scores, axis=0, keepdims=True)
                weights = jnp.exp2((scores - top) * EXP2_SCALE)
                probs = weights * (1.0 / jnp.sum(weights, axis=0, keepdims=True))
                dprobs = lax.dot_general(value, grad, TRANS_B, preferred_element_type=jnp.float32)
                delta = jnp.sum(probs * dprobs, axis=0, keepdims=True)
                dscores = (probs * (dprobs - delta)).astype(jnp.bfloat16)
                probs_low = probs.astype(jnp.bfloat16)
                grad_query = lax.dot_general(
                    dscores, key, TRANS_A, preferred_element_type=jnp.float32
                )
                grad_query = (grad_query * SCALE).astype(jnp.bfloat16)
                for k, i in enumerate(heads):
                    gq_ref[here, lanes(i, HD)] = grad_query[k * BLK : (k + 1) * BLK]
                key_term = jnp.dot(dscores, query, preferred_element_type=jnp.float32)
                value_term = jnp.dot(probs_low, grad, preferred_element_type=jnp.float32)
                grad_key = key_term if grad_key is None else grad_key + key_term
                grad_value = value_term if grad_value is None else grad_value + value_term
            shared = slice(b * BLK, b * BLK + rows)
            fresh = slice(b * BLK + rows, b * BLK + span)
            for total, term in ((dk_ref, grad_key), (dv_ref, grad_value)):
                if b == 0:
                    total[h, shared, :] = term[:rows]
                else:
                    total[h, shared, :] += term[:rows]
                total[h, fresh, :] = term[rows:]

        back_send[h, 0] = (dk_ref[h, 0:rows, :] * SCALE).astype(jnp.bfloat16)
        back_send[h, 1] = dv_ref[h, 0:rows, :].astype(jnp.bfloat16)

        @pl.when(has_prev)
        def _():
            back_copy(h).start()

        return carry

    lax.fori_loop(0, HK, head_step, 0)

    @pl.when(jnp.logical_not(has_next))
    def _():
        back_recv[...] = jnp.zeros_like(back_recv)

    for h in range(HK):

        @pl.when(has_next)
        def _():
            back_copy(h).wait_recv()

        columns = slice(h * HD, (h + 1) * HD)
        gk_ref[:, columns] = (
            dk_ref[h, rows:, :] * SCALE + back_recv[h, 0].astype(jnp.float32)
        ).astype(jnp.bfloat16)
        gv_ref[:, columns] = (
            dv_ref[h, rows:, :] + back_recv[h, 1].astype(jnp.float32)
        ).astype(jnp.bfloat16)

    @pl.when(has_next)
    def _():
        chan_copy.wait_send()
        for h in range(HK):
            for copy in forward_copies(h):
                copy.wait_send()

    @pl.when(has_prev)
    def _():
        for h in range(HK):
            back_copy(h).wait_send()


def per_device(queries, keys, values, grad_out, seg_starts, channels):
    rows = queries.shape[0]
    blocks = rows // BLK
    span = rows + BLK
    vmem = pl.BlockSpec(memory_space=pltpu.VMEM)
    hbm = pl.BlockSpec(memory_space=pl.ANY)
    return pl.pallas_call(
        functools.partial(kernel, lax.axis_size("ctx")),
        out_shape=(
            jax.ShapeDtypeStruct(queries.shape, jnp.bfloat16),
            jax.ShapeDtypeStruct(keys.shape, jnp.bfloat16),
            jax.ShapeDtypeStruct(values.shape, jnp.bfloat16),
        ),
        in_specs=[pl.BlockSpec(memory_space=pltpu.SMEM), vmem, hbm, hbm, hbm, hbm],
        out_specs=(vmem, vmem, vmem),
        scratch_shapes=[
            pltpu.VMEM((rows, HQ * HD), jnp.bfloat16),
            pltpu.VMEM((rows, HQ * HD), jnp.bfloat16),
            pltpu.VMEM((2 * rows, HK * HD), jnp.bfloat16),
            pltpu.VMEM((2 * rows, HK * HD), jnp.bfloat16),
            pltpu.VMEM((1, rows), jnp.int32),
            pltpu.VMEM((blocks, span, BLK), jnp.float32),
            pltpu.VMEM((HK, 2 * rows, HD), jnp.float32),
            pltpu.VMEM((HK, 2 * rows, HD), jnp.float32),
            pltpu.VMEM((HK, 2, rows, HD), jnp.bfloat16),
            pltpu.VMEM((HK, 2, rows, HD), jnp.bfloat16),
            pltpu.SemaphoreType.DMA((4, HK)),
            pltpu.SemaphoreType.DMA((2, HK)),
            pltpu.SemaphoreType.DMA((2, HK)),
            pltpu.SemaphoreType.DMA((2,)),
            pltpu.SemaphoreType.DMA((HK,)),
            pltpu.SemaphoreType.DMA((HK,)),
        ],
        compiler_params=pltpu.CompilerParams(
            collective_id=0, has_side_effects=True, vmem_limit_bytes=56 * 1024 * 1024
        ),
        name="window_backward",
    )(seg_starts, channels.reshape(1, rows), queries, keys, values, grad_out)


def solution(mesh):
    placed = (
        P(("groups", "ctx"), None),
        P(("groups", "ctx"), None),
        P(("groups", "ctx"), None),
        P(("groups", "ctx"), None),
        P("groups"),
        P(("groups", "ctx")),
    )
    return jax.shard_map(
        per_device,
        mesh=mesh,
        in_specs=placed,
        out_specs=(
            P(("groups", "ctx"), None),
            P(("groups", "ctx"), None),
            P(("groups", "ctx"), None),
        ),
        check_vma=False,
    )
```

```python
import functools

import jax
import jax.numpy as jnp
import numpy as np
from jax import lax
from jax.experimental import pallas as pl
from jax.experimental.pallas import tpu as pltpu
from jax.sharding import PartitionSpec as P

HQ = 16
HK = 4
HD = 128
LAG = 16
GROUP = HQ // HK
BLK = 128
MASKED = -1e30
SCALE = HD ** (-0.5)
EXP2_SCALE = float(SCALE * np.log2(np.e))

TRANS_B = (((1,), (1,)), ((), ()))
TRANS_A = (((0,), (0,)), ((), ()))


def kernel(
    count,
    seg_ref,
    chan_ref,
    q_hbm,
    k_hbm,
    v_hbm,
    g_hbm,
    gq_ref,
    gk_ref,
    gv_ref,
    q_ref,
    g_ref,
    kw_ref,
    vw_ref,
    chan_prev,
    bias_ref,
    dk_ref,
    dv_ref,
    back_send,
    back_recv,
    local_sem,
    fwd_send_sem,
    fwd_recv_sem,
    chan_sem,
    back_send_sem,
    back_recv_sem,
):
    rows = q_ref.shape[0]
    blocks = rows // BLK
    span = rows + BLK
    me = lax.axis_index("ctx")
    has_prev = me > 0
    has_next = me < count - 1

    def lanes(h, width):
        return pl.ds(pl.multiple_of(h * width, width), width)

    def local_copies(h):
        own = pl.ds(rows, rows)
        return (
            pltpu.make_async_copy(
                k_hbm.at[:, lanes(h, HD)], kw_ref.at[own, lanes(h, HD)], local_sem.at[0, h]
            ),
            pltpu.make_async_copy(
                v_hbm.at[:, lanes(h, HD)], vw_ref.at[own, lanes(h, HD)], local_sem.at[1, h]
            ),
            pltpu.make_async_copy(
                q_hbm.at[:, lanes(h, GROUP * HD)], q_ref.at[:, lanes(h, GROUP * HD)], local_sem.at[2, h]
            ),
            pltpu.make_async_copy(
                g_hbm.at[:, lanes(h, GROUP * HD)], g_ref.at[:, lanes(h, GROUP * HD)], local_sem.at[3, h]
            ),
        )

    def forward_copies(h):
        before = pl.ds(0, rows)
        return tuple(
            pltpu.make_async_remote_copy(
                src_ref=source.at[:, lanes(h, HD)],
                dst_ref=window.at[before, lanes(h, HD)],
                send_sem=fwd_send_sem.at[which, h],
                recv_sem=fwd_recv_sem.at[which, h],
                device_id={"ctx": me + 1},
                device_id_type=pl.DeviceIdType.MESH,
            )
            for which, (source, window) in enumerate(((k_hbm, kw_ref), (v_hbm, vw_ref)))
        )

    chan_copy = pltpu.make_async_remote_copy(
        src_ref=chan_ref,
        dst_ref=chan_prev,
        send_sem=chan_sem.at[0],
        recv_sem=chan_sem.at[1],
        device_id={"ctx": me + 1},
        device_id_type=pl.DeviceIdType.MESH,
    )

    def back_copy(h):
        return pltpu.make_async_remote_copy(
            src_ref=back_send.at[h],
            dst_ref=back_recv.at[h],
            send_sem=back_send_sem.at[h],
            recv_sem=back_recv_sem.at[h],
            device_id={"ctx": me - 1},
            device_id_type=pl.DeviceIdType.MESH,
        )

    barrier = pltpu.get_barrier_semaphore()

    @pl.when(has_prev)
    def _():
        pl.semaphore_signal(
            barrier, inc=1, device_id={"ctx": me - 1}, device_id_type=pl.DeviceIdType.MESH
        )

    @pl.when(has_next)
    def _():
        pl.semaphore_signal(
            barrier, inc=1, device_id={"ctx": me + 1}, device_id_type=pl.DeviceIdType.MESH
        )

    for h in range(HK):
        for copy in local_copies(h):
            copy.start()
    pl.semaphore_wait(barrier, has_prev.astype(jnp.int32) + has_next.astype(jnp.int32))

    @pl.when(has_next)
    def _():
        chan_copy.start()
        for copy in forward_copies(0):
            copy.start()

    @pl.when(jnp.logical_not(has_prev))
    def _():
        kw_ref[0:rows, :] = jnp.zeros((rows, HK * HD), jnp.bfloat16)
        vw_ref[0:rows, :] = jnp.zeros((rows, HK * HD), jnp.bfloat16)
        chan_prev[...] = jnp.zeros_like(chan_prev)

    @pl.when(has_prev)
    def _():
        chan_copy.wait_recv()

    def column(row):
        return jnp.transpose(jnp.broadcast_to(row, (BLK, BLK)))

    first_row = me * rows
    for b in range(blocks):
        here = slice(b * BLK, (b + 1) * BLK)
        position = first_row + b * BLK + lax.broadcasted_iota(jnp.int32, (1, BLK), 1)
        start = jnp.zeros((1, BLK), jnp.int32)
        for s in range(seg_ref.shape[0]):
            start = jnp.maximum(start, jnp.where(seg_ref[s] <= position, seg_ref[s], 0))
        start = start - (first_row - rows + b * BLK)
        query_chan = chan_ref[:, here]
        query = lax.broadcasted_iota(jnp.int32, (BLK, BLK), 1)
        for c in range(span // BLK):
            key = c * BLK + lax.broadcasted_iota(jnp.int32, (BLK, BLK), 0)
            place = (b + c) * BLK
            if place < rows:
                key_chan = chan_prev[:, place : place + BLK]
            else:
                key_chan = chan_ref[:, place - rows : place - rows + BLK]
            allowed = (key > query) & (key <= query + rows) & (key >= start)
            allowed = allowed & (
                (column(key_chan) == query_chan) | (key <= query + (rows - LAG))
            )
            bias_ref[b, c * BLK : (c + 1) * BLK, :] = jnp.where(allowed, 0.0, MASKED)

    def head_step(h, carry):
        for copy in local_copies(h):
            copy.wait()

        @pl.when(has_prev)
        def _():
            for copy in forward_copies(h):
                copy.wait_recv()

        @pl.when(has_next & (h == 0))
        def _():
            for ahead in range(1, min(3, HK)):
                for copy in forward_copies(ahead):
                    copy.start()

        @pl.when(has_next & (h > 0) & (h < HK - 2))
        def _():
            for copy in forward_copies(h + 2):
                copy.start()

        units = [(b, pair) for b in range(blocks) for pair in range(GROUP // 2)]

        def products(unit):
            b, pair = unit
            here = slice(b * BLK, (b + 1) * BLK)
            window = slice(b * BLK, b * BLK + span)
            heads = [h * GROUP + 2 * pair, h * GROUP + 2 * pair + 1]
            key = kw_ref[window, lanes(h, HD)]
            value = vw_ref[window, lanes(h, HD)]
            query = jnp.concatenate([q_ref[here, lanes(i, HD)] for i in heads], axis=0)
            grad = jnp.concatenate([g_ref[here, lanes(i, HD)] for i in heads], axis=0)
            scores = lax.dot_general(key, query, TRANS_B, preferred_element_type=jnp.float32)
            dprobs = lax.dot_general(value, grad, TRANS_B, preferred_element_type=jnp.float32)
            return scores, dprobs

        def softmax(unit, scores, dprobs):
            bias = bias_ref[unit[0]]
            scores = scores + jnp.concatenate([bias, bias], axis=1)
            top = jnp.max(scores, axis=0, keepdims=True)
            weights = jnp.exp2((scores - top) * EXP2_SCALE)
            probs = weights * (1.0 / jnp.sum(weights, axis=0, keepdims=True))
            delta = jnp.sum(probs * dprobs, axis=0, keepdims=True)
            dscores = (probs * (dprobs - delta)).astype(jnp.bfloat16)
            return dscores, probs.astype(jnp.bfloat16)

        def gradients(unit, dscores, probs_low):
            b, pair = unit
            here = slice(b * BLK, (b + 1) * BLK)
            window = slice(b * BLK, b * BLK + span)
            heads = [h * GROUP + 2 * pair, h * GROUP + 2 * pair + 1]
            key = kw_ref[window, lanes(h, HD)]
            query = jnp.concatenate([q_ref[here, lanes(i, HD)] for i in heads], axis=0)
            grad = jnp.concatenate([g_ref[here, lanes(i, HD)] for i in heads], axis=0)
            grad_query = lax.dot_general(key, dscores, TRANS_A, preferred_element_type=jnp.float32)
            grad_query = jnp.transpose((grad_query * SCALE).astype(jnp.bfloat16))
            for k, i in enumerate(heads):
                gq_ref[here, lanes(i, HD)] = grad_query[k * BLK : (k + 1) * BLK]
            key_term = jnp.dot(dscores, query, preferred_element_type=jnp.float32)
            value_term = jnp.dot(probs_low, grad, preferred_element_type=jnp.float32)
            shared = slice(b * BLK, b * BLK + rows)
            fresh = slice(b * BLK + rows, b * BLK + span)
            for total, term in ((dk_ref, key_term), (dv_ref, value_term)):
                if unit == (0, 0):
                    total[h, 0:span, :] = term
                elif pair == 0:
                    total[h, shared, :] += term[:rows]
                    total[h, fresh, :] = term[rows:]
                else:
                    total[h, b * BLK : b * BLK + span, :] += term

        ready = products(units[0])
        done = None
        for at, unit in enumerate(units):
            later = products(units[at + 1]) if at + 1 < len(units) else None
            low = softmax(unit, *ready)
            if done is not None:
                gradients(*done)
            done = (unit, *low)
            ready = later
        gradients(*done)

        back_send[h, 0] = (dk_ref[h, 0:rows, :] * SCALE).astype(jnp.bfloat16)
        back_send[h, 1] = dv_ref[h, 0:rows, :].astype(jnp.bfloat16)

        @pl.when(has_prev)
        def _():
            back_copy(h).start()

        return carry

    lax.fori_loop(0, HK, head_step, 0)

    @pl.when(jnp.logical_not(has_next))
    def _():
        back_recv[...] = jnp.zeros_like(back_recv)

    for h in range(HK):

        @pl.when(has_next)
        def _():
            back_copy(h).wait_recv()

        columns = slice(h * HD, (h + 1) * HD)
        gk_ref[:, columns] = (
            dk_ref[h, rows:, :] * SCALE + back_recv[h, 0].astype(jnp.float32)
        ).astype(jnp.bfloat16)
        gv_ref[:, columns] = (
            dv_ref[h, rows:, :] + back_recv[h, 1].astype(jnp.float32)
        ).astype(jnp.bfloat16)

    @pl.when(has_next)
    def _():
        chan_copy.wait_send()
        for h in range(HK):
            for copy in forward_copies(h):
                copy.wait_send()

    @pl.when(has_prev)
    def _():
        for h in range(HK):
            back_copy(h).wait_send()


def per_device(queries, keys, values, grad_out, seg_starts, channels):
    rows = queries.shape[0]
    blocks = rows // BLK
    span = rows + BLK
    vmem = pl.BlockSpec(memory_space=pltpu.VMEM)
    hbm = pl.BlockSpec(memory_space=pl.ANY)
    return pl.pallas_call(
        functools.partial(kernel, lax.axis_size("ctx")),
        out_shape=(
            jax.ShapeDtypeStruct(queries.shape, jnp.bfloat16),
            jax.ShapeDtypeStruct(keys.shape, jnp.bfloat16),
            jax.ShapeDtypeStruct(values.shape, jnp.bfloat16),
        ),
        in_specs=[pl.BlockSpec(memory_space=pltpu.SMEM), vmem, hbm, hbm, hbm, hbm],
        out_specs=(vmem, vmem, vmem),
        scratch_shapes=[
            pltpu.VMEM((rows, HQ * HD), jnp.bfloat16),
            pltpu.VMEM((rows, HQ * HD), jnp.bfloat16),
            pltpu.VMEM((2 * rows, HK * HD), jnp.bfloat16),
            pltpu.VMEM((2 * rows, HK * HD), jnp.bfloat16),
            pltpu.VMEM((1, rows), jnp.int32),
            pltpu.VMEM((blocks, span, BLK), jnp.float32),
            pltpu.VMEM((HK, 2 * rows, HD), jnp.float32),
            pltpu.VMEM((HK, 2 * rows, HD), jnp.float32),
            pltpu.VMEM((HK, 2, rows, HD), jnp.bfloat16),
            pltpu.VMEM((HK, 2, rows, HD), jnp.bfloat16),
            pltpu.SemaphoreType.DMA((4, HK)),
            pltpu.SemaphoreType.DMA((2, HK)),
            pltpu.SemaphoreType.DMA((2, HK)),
            pltpu.SemaphoreType.DMA((2,)),
            pltpu.SemaphoreType.DMA((HK,)),
            pltpu.SemaphoreType.DMA((HK,)),
        ],
        compiler_params=pltpu.CompilerParams(
            collective_id=0, has_side_effects=True, vmem_limit_bytes=56 * 1024 * 1024
        ),
        name="window_backward",
    )(seg_starts, channels.reshape(1, rows), queries, keys, values, grad_out)


def solution(mesh):
    placed = (
        P(("groups", "ctx"), None),
        P(("groups", "ctx"), None),
        P(("groups", "ctx"), None),
        P(("groups", "ctx"), None),
        P("groups"),
        P(("groups", "ctx")),
    )
    return jax.shard_map(
        per_device,
        mesh=mesh,
        in_specs=placed,
        out_specs=(
            P(("groups", "ctx"), None),
            P(("groups", "ctx"), None),
            P(("groups", "ctx"), None),
        ),
        check_vma=False,
    )
```

```python
import functools

import jax
import jax.numpy as jnp
import numpy as np
from jax import lax
from jax.experimental import pallas as pl
from jax.experimental.pallas import tpu as pltpu
from jax.sharding import PartitionSpec as P

HQ = 16
HK = 4
HD = 128
LAG = 16
GROUP = HQ // HK
BLK = 128
MASKED = -1e30
SCALE = HD ** (-0.5)
EXP2_SCALE = float(SCALE * np.log2(np.e))

TRANS_B = (((1,), (1,)), ((), ()))
TRANS_A = (((0,), (0,)), ((), ()))


def kernel(
    count,
    seg_ref,
    chan_ref,
    q_hbm,
    k_hbm,
    v_hbm,
    g_hbm,
    gq_ref,
    gk_ref,
    gv_ref,
    q_ref,
    g_ref,
    kw_ref,
    vw_ref,
    chan_prev,
    bias_ref,
    dk_ref,
    dv_ref,
    back_send,
    back_recv,
    local_sem,
    fwd_send_sem,
    fwd_recv_sem,
    chan_sem,
    back_send_sem,
    back_recv_sem,
):
    rows = q_ref.shape[0]
    blocks = rows // BLK
    span = rows + BLK
    me = lax.axis_index("ctx")
    has_prev = me > 0
    has_next = me < count - 1

    def lanes(h, width):
        return pl.ds(pl.multiple_of(h * width, width), width)

    def local_copies(h):
        own = pl.ds(rows, rows)
        return (
            pltpu.make_async_copy(
                k_hbm.at[:, lanes(h, HD)], kw_ref.at[own, lanes(h, HD)], local_sem.at[0, h]
            ),
            pltpu.make_async_copy(
                v_hbm.at[:, lanes(h, HD)], vw_ref.at[own, lanes(h, HD)], local_sem.at[1, h]
            ),
            pltpu.make_async_copy(
                q_hbm.at[:, lanes(h, GROUP * HD)], q_ref.at[:, lanes(h, GROUP * HD)], local_sem.at[2, h]
            ),
            pltpu.make_async_copy(
                g_hbm.at[:, lanes(h, GROUP * HD)], g_ref.at[:, lanes(h, GROUP * HD)], local_sem.at[3, h]
            ),
        )

    def forward_copies(h):
        before = pl.ds(0, rows)
        return tuple(
            pltpu.make_async_remote_copy(
                src_ref=source.at[:, lanes(h, HD)],
                dst_ref=window.at[before, lanes(h, HD)],
                send_sem=fwd_send_sem.at[which, h],
                recv_sem=fwd_recv_sem.at[which, h],
                device_id={"ctx": me + 1},
                device_id_type=pl.DeviceIdType.MESH,
            )
            for which, (source, window) in enumerate(((k_hbm, kw_ref), (v_hbm, vw_ref)))
        )

    chan_copy = pltpu.make_async_remote_copy(
        src_ref=chan_ref,
        dst_ref=chan_prev,
        send_sem=chan_sem.at[0],
        recv_sem=chan_sem.at[1],
        device_id={"ctx": me + 1},
        device_id_type=pl.DeviceIdType.MESH,
    )

    def back_copy(h):
        return pltpu.make_async_remote_copy(
            src_ref=back_send.at[h],
            dst_ref=back_recv.at[h],
            send_sem=back_send_sem.at[h],
            recv_sem=back_recv_sem.at[h],
            device_id={"ctx": me - 1},
            device_id_type=pl.DeviceIdType.MESH,
        )

    barrier = pltpu.get_barrier_semaphore()

    @pl.when(has_prev)
    def _():
        pl.semaphore_signal(
            barrier, inc=1, device_id={"ctx": me - 1}, device_id_type=pl.DeviceIdType.MESH
        )

    @pl.when(has_next)
    def _():
        pl.semaphore_signal(
            barrier, inc=1, device_id={"ctx": me + 1}, device_id_type=pl.DeviceIdType.MESH
        )

    for h in range(HK):
        for copy in local_copies(h):
            copy.start()
    pl.semaphore_wait(barrier, has_prev.astype(jnp.int32) + has_next.astype(jnp.int32))

    @pl.when(has_next)
    def _():
        chan_copy.start()
        for copy in forward_copies(0):
            copy.start()

    @pl.when(jnp.logical_not(has_prev))
    def _():
        kw_ref[0:rows, :] = jnp.zeros((rows, HK * HD), jnp.bfloat16)
        vw_ref[0:rows, :] = jnp.zeros((rows, HK * HD), jnp.bfloat16)
        chan_prev[...] = jnp.zeros_like(chan_prev)

    @pl.when(has_prev)
    def _():
        chan_copy.wait_recv()

    def column(row):
        return jnp.transpose(jnp.broadcast_to(row, (BLK, BLK)))

    first_row = me * rows
    for b in range(blocks):
        here = slice(b * BLK, (b + 1) * BLK)
        position = first_row + b * BLK + lax.broadcasted_iota(jnp.int32, (1, BLK), 1)
        start = jnp.zeros((1, BLK), jnp.int32)
        for s in range(seg_ref.shape[0]):
            start = jnp.maximum(start, jnp.where(seg_ref[s] <= position, seg_ref[s], 0))
        start = start - (first_row - rows + b * BLK)
        query_chan = chan_ref[:, here]
        query = lax.broadcasted_iota(jnp.int32, (BLK, BLK), 1)
        for c in range(span // BLK):
            key = c * BLK + lax.broadcasted_iota(jnp.int32, (BLK, BLK), 0)
            place = (b + c) * BLK
            if place < rows:
                key_chan = chan_prev[:, place : place + BLK]
            else:
                key_chan = chan_ref[:, place - rows : place - rows + BLK]
            allowed = (key > query) & (key <= query + rows) & (key >= start)
            allowed = allowed & (
                (column(key_chan) == query_chan) | (key <= query + (rows - LAG))
            )
            bias_ref[b, c * BLK : (c + 1) * BLK, :] = jnp.where(allowed, 0.0, MASKED)

    def head_step(h, carry):
        for copy in local_copies(h):
            copy.wait()

        @pl.when(has_prev)
        def _():
            for copy in forward_copies(h):
                copy.wait_recv()

        @pl.when(has_next & (h == 0))
        def _():
            for ahead in range(1, min(3, HK)):
                for copy in forward_copies(ahead):
                    copy.start()

        @pl.when(has_next & (h > 0) & (h < HK - 2))
        def _():
            for copy in forward_copies(h + 2):
                copy.start()

        units = [(b, pair) for b in range(blocks) for pair in range(GROUP // 2)]

        def products(unit):
            b, pair = unit
            here = slice(b * BLK, (b + 1) * BLK)
            window = slice(b * BLK, b * BLK + span)
            heads = [h * GROUP + 2 * pair, h * GROUP + 2 * pair + 1]
            key = kw_ref[window, lanes(h, HD)]
            value = vw_ref[window, lanes(h, HD)]
            query = jnp.concatenate([q_ref[here, lanes(i, HD)] for i in heads], axis=0)
            grad = jnp.concatenate([g_ref[here, lanes(i, HD)] for i in heads], axis=0)
            scores = lax.dot_general(key, query, TRANS_B, preferred_element_type=jnp.float32)
            dprobs = lax.dot_general(value, grad, TRANS_B, preferred_element_type=jnp.float32)
            return scores, dprobs

        def softmax(unit, scores, dprobs):
            bias = bias_ref[unit[0]]
            scores = scores + jnp.concatenate([bias, bias], axis=1)
            top = jnp.max(scores, axis=0, keepdims=True)
            weights = jnp.exp2((scores - top) * EXP2_SCALE)
            probs = weights * (1.0 / jnp.sum(weights, axis=0, keepdims=True))
            delta = jnp.sum(probs * dprobs, axis=0, keepdims=True)
            dscores = (probs * (dprobs - delta)).astype(jnp.bfloat16)
            return dscores, probs.astype(jnp.bfloat16)

        def gradients(unit, dscores, probs_low):
            b, pair = unit
            here = slice(b * BLK, (b + 1) * BLK)
            window = slice(b * BLK, b * BLK + span)
            heads = [h * GROUP + 2 * pair, h * GROUP + 2 * pair + 1]
            key = kw_ref[window, lanes(h, HD)]
            query = jnp.concatenate([q_ref[here, lanes(i, HD)] for i in heads], axis=0)
            grad = jnp.concatenate([g_ref[here, lanes(i, HD)] for i in heads], axis=0)
            grad_query = lax.dot_general(key, dscores, TRANS_A, preferred_element_type=jnp.float32)
            grad_query = jnp.transpose((grad_query * SCALE).astype(jnp.bfloat16))
            for k, i in enumerate(heads):
                gq_ref[here, lanes(i, HD)] = grad_query[k * BLK : (k + 1) * BLK]
            key_term = jnp.dot(dscores, query, preferred_element_type=jnp.float32)
            value_term = jnp.dot(probs_low, grad, preferred_element_type=jnp.float32)
            shared = slice(b * BLK, b * BLK + rows)
            fresh = slice(b * BLK + rows, b * BLK + span)
            for total, term in ((dk_ref, key_term), (dv_ref, value_term)):
                if unit == (0, 0):
                    total[h, 0:span, :] = term
                elif pair == 0:
                    total[h, shared, :] += term[:rows]
                    total[h, fresh, :] = term[rows:]
                else:
                    total[h, b * BLK : b * BLK + span, :] += term

        ready = products(units[0])
        done = None
        for at, unit in enumerate(units):
            later = products(units[at + 1]) if at + 1 < len(units) else None
            low = softmax(unit, *ready)
            if done is not None:
                gradients(*done)
            done = (unit, *low)
            ready = later
        gradients(*done)

        back_send[h, 0] = (dk_ref[h, 0:rows, :] * SCALE).astype(jnp.bfloat16)
        back_send[h, 1] = dv_ref[h, 0:rows, :].astype(jnp.bfloat16)

        @pl.when(has_prev)
        def _():
            back_copy(h).start()

        return carry

    lax.fori_loop(0, HK, head_step, 0)

    @pl.when(jnp.logical_not(has_next))
    def _():
        back_recv[...] = jnp.zeros_like(back_recv)

    for h in range(HK):

        @pl.when(has_next)
        def _():
            back_copy(h).wait_recv()

        columns = slice(h * HD, (h + 1) * HD)
        gk_ref[:, columns] = (
            dk_ref[h, rows:, :] * SCALE + back_recv[h, 0].astype(jnp.float32)
        ).astype(jnp.bfloat16)
        gv_ref[:, columns] = (
            dv_ref[h, rows:, :] + back_recv[h, 1].astype(jnp.float32)
        ).astype(jnp.bfloat16)

    @pl.when(has_next)
    def _():
        chan_copy.wait_send()
        for h in range(HK):
            for copy in forward_copies(h):
                copy.wait_send()

    @pl.when(has_prev)
    def _():
        for h in range(HK):
            back_copy(h).wait_send()


def store(gq_ref, gk_ref, gv_ref, gq_hbm, gk_hbm, gv_hbm, sem):
    copies = [
        pltpu.make_async_copy(source, target, sem.at[at])
        for at, (source, target) in enumerate(
            ((gq_ref, gq_hbm), (gk_ref, gk_hbm), (gv_ref, gv_hbm))
        )
    ]
    for copy in copies:
        copy.start()
    for copy in copies:
        copy.wait()


def per_device(queries, keys, values, grad_out, seg_starts, channels):
    rows = queries.shape[0]
    blocks = rows // BLK
    span = rows + BLK
    vmem = pl.BlockSpec(memory_space=pltpu.VMEM)
    hbm = pl.BlockSpec(memory_space=pl.ANY)
    held = pl.pallas_call(
        functools.partial(kernel, lax.axis_size("ctx")),
        out_shape=(
            pltpu.VMEM(queries.shape, jnp.bfloat16),
            pltpu.VMEM(keys.shape, jnp.bfloat16),
            pltpu.VMEM(values.shape, jnp.bfloat16),
        ),
        in_specs=[pl.BlockSpec(memory_space=pltpu.SMEM), vmem, hbm, hbm, hbm, hbm],
        out_specs=(vmem, vmem, vmem),
        scratch_shapes=[
            pltpu.VMEM((rows, HQ * HD), jnp.bfloat16),
            pltpu.VMEM((rows, HQ * HD), jnp.bfloat16),
            pltpu.VMEM((2 * rows, HK * HD), jnp.bfloat16),
            pltpu.VMEM((2 * rows, HK * HD), jnp.bfloat16),
            pltpu.VMEM((1, rows), jnp.int32),
            pltpu.VMEM((blocks, span, BLK), jnp.float32),
            pltpu.VMEM((HK, 2 * rows, HD), jnp.float32),
            pltpu.VMEM((HK, 2 * rows, HD), jnp.float32),
            pltpu.VMEM((HK, 2, rows, HD), jnp.bfloat16),
            pltpu.VMEM((HK, 2, rows, HD), jnp.bfloat16),
            pltpu.SemaphoreType.DMA((4, HK)),
            pltpu.SemaphoreType.DMA((2, HK)),
            pltpu.SemaphoreType.DMA((2, HK)),
            pltpu.SemaphoreType.DMA((2,)),
            pltpu.SemaphoreType.DMA((HK,)),
            pltpu.SemaphoreType.DMA((HK,)),
        ],
        compiler_params=pltpu.CompilerParams(
            collective_id=0, has_side_effects=True, vmem_limit_bytes=60 * 1024 * 1024
        ),
        name="window_backward",
    )(seg_starts, channels.reshape(1, rows), queries, keys, values, grad_out)
    return pl.pallas_call(
        store,
        out_shape=tuple(jax.ShapeDtypeStruct(x.shape, x.dtype) for x in (queries, keys, values)),
        in_specs=[pl.BlockSpec(memory_space=pl.ANY)] * 3,
        out_specs=(hbm,) * 3,
        scratch_shapes=[pltpu.SemaphoreType.DMA((3,))],
        compiler_params=pltpu.CompilerParams(vmem_limit_bytes=2 * 1024 * 1024),
        name="store",
    )(*held)


def solution(mesh):
    placed = (
        P(("groups", "ctx"), None),
        P(("groups", "ctx"), None),
        P(("groups", "ctx"), None),
        P(("groups", "ctx"), None),
        P("groups"),
        P(("groups", "ctx")),
    )
    return jax.shard_map(
        per_device,
        mesh=mesh,
        in_specs=placed,
        out_specs=(
            P(("groups", "ctx"), None),
            P(("groups", "ctx"), None),
            P(("groups", "ctx"), None),
        ),
        check_vma=False,
    )
```

```python
import functools

import jax
import jax.numpy as jnp
import numpy as np
from jax import lax
from jax.experimental import pallas as pl
from jax.experimental.pallas import tpu as pltpu
from jax.sharding import PartitionSpec as P

HQ = 16
HK = 4
HD = 128
LAG = 16
GROUP = HQ // HK
BLK = 128
MASKED = -1e30
SCALE = HD ** (-0.5)
EXP2_SCALE = float(SCALE * np.log2(np.e))

TRANS_B = (((1,), (1,)), ((), ()))
TRANS_A = (((0,), (0,)), ((), ()))


def kernel(
    count,
    seg_ref,
    chan_ref,
    q_hbm,
    k_hbm,
    v_hbm,
    g_hbm,
    gq_ref,
    gk_ref,
    gv_ref,
    q_ref,
    g_ref,
    kw_ref,
    vw_ref,
    chan_prev,
    bias_ref,
    dk_ref,
    dv_ref,
    back_send,
    back_recv,
    local_sem,
    fwd_send_sem,
    fwd_recv_sem,
    chan_sem,
    back_send_sem,
    back_recv_sem,
):
    rows = q_ref.shape[0]
    blocks = rows // BLK
    span = rows + BLK
    me = lax.axis_index("ctx")
    has_prev = me > 0
    has_next = me < count - 1

    def lanes(h, width):
        return pl.ds(pl.multiple_of(h * width, width), width)

    def local_copies(h):
        own = pl.ds(rows, rows)
        return (
            pltpu.make_async_copy(
                k_hbm.at[:, lanes(h, HD)], kw_ref.at[own, lanes(h, HD)], local_sem.at[0, h]
            ),
            pltpu.make_async_copy(
                v_hbm.at[:, lanes(h, HD)], vw_ref.at[own, lanes(h, HD)], local_sem.at[1, h]
            ),
            pltpu.make_async_copy(
                q_hbm.at[:, lanes(h, GROUP * HD)], q_ref.at[:, lanes(h, GROUP * HD)], local_sem.at[2, h]
            ),
            pltpu.make_async_copy(
                g_hbm.at[:, lanes(h, GROUP * HD)], g_ref.at[:, lanes(h, GROUP * HD)], local_sem.at[3, h]
            ),
        )

    def forward_copies(h):
        before = pl.ds(0, rows)
        return tuple(
            pltpu.make_async_remote_copy(
                src_ref=source.at[:, lanes(h, HD)],
                dst_ref=window.at[before, lanes(h, HD)],
                send_sem=fwd_send_sem.at[which, h],
                recv_sem=fwd_recv_sem.at[which, h],
                device_id={"ctx": me + 1},
                device_id_type=pl.DeviceIdType.MESH,
            )
            for which, (source, window) in enumerate(((k_hbm, kw_ref), (v_hbm, vw_ref)))
        )

    chan_copy = pltpu.make_async_remote_copy(
        src_ref=chan_ref,
        dst_ref=chan_prev,
        send_sem=chan_sem.at[0],
        recv_sem=chan_sem.at[1],
        device_id={"ctx": me + 1},
        device_id_type=pl.DeviceIdType.MESH,
    )

    def back_copy(h):
        return pltpu.make_async_remote_copy(
            src_ref=back_send.at[h],
            dst_ref=back_recv.at[h],
            send_sem=back_send_sem.at[h],
            recv_sem=back_recv_sem.at[h],
            device_id={"ctx": me - 1},
            device_id_type=pl.DeviceIdType.MESH,
        )

    barrier = pltpu.get_barrier_semaphore()

    @pl.when(has_prev)
    def _():
        pl.semaphore_signal(
            barrier, inc=1, device_id={"ctx": me - 1}, device_id_type=pl.DeviceIdType.MESH
        )

    @pl.when(has_next)
    def _():
        pl.semaphore_signal(
            barrier, inc=1, device_id={"ctx": me + 1}, device_id_type=pl.DeviceIdType.MESH
        )

    for h in range(HK):
        for copy in local_copies(h):
            copy.start()
    pl.semaphore_wait(barrier, has_prev.astype(jnp.int32) + has_next.astype(jnp.int32))

    @pl.when(has_next)
    def _():
        chan_copy.start()
        for copy in forward_copies(0):
            copy.start()

    @pl.when(jnp.logical_not(has_prev))
    def _():
        kw_ref[0:rows, :] = jnp.zeros((rows, HK * HD), jnp.bfloat16)
        vw_ref[0:rows, :] = jnp.zeros((rows, HK * HD), jnp.bfloat16)
        chan_prev[...] = jnp.zeros_like(chan_prev)

    @pl.when(has_prev)
    def _():
        chan_copy.wait_recv()

    def column(row):
        return jnp.transpose(jnp.broadcast_to(row, (BLK, BLK)))

    first_row = me * rows
    for b in range(blocks):
        here = slice(b * BLK, (b + 1) * BLK)
        position = first_row + b * BLK + lax.broadcasted_iota(jnp.int32, (1, BLK), 1)
        start = jnp.zeros((1, BLK), jnp.int32)
        for s in range(seg_ref.shape[0]):
            start = jnp.maximum(start, jnp.where(seg_ref[s] <= position, seg_ref[s], 0))
        start = start - (first_row - rows + b * BLK)
        query_chan = chan_ref[:, here]
        query = lax.broadcasted_iota(jnp.int32, (BLK, BLK), 1)
        for c in range(span // BLK):
            key = c * BLK + lax.broadcasted_iota(jnp.int32, (BLK, BLK), 0)
            place = (b + c) * BLK
            if place < rows:
                key_chan = chan_prev[:, place : place + BLK]
            else:
                key_chan = chan_ref[:, place - rows : place - rows + BLK]
            allowed = (key > query) & (key <= query + rows) & (key >= start)
            allowed = allowed & (
                (column(key_chan) == query_chan) | (key <= query + (rows - LAG))
            )
            bias_ref[b, c * BLK : (c + 1) * BLK, :] = jnp.where(allowed, 0.0, MASKED)

    def head_step(h, carry):
        for copy in local_copies(h):
            copy.wait()

        @pl.when(has_prev)
        def _():
            for copy in forward_copies(h):
                copy.wait_recv()

        @pl.when(has_next & (h == 0))
        def _():
            for ahead in range(1, min(3, HK)):
                for copy in forward_copies(ahead):
                    copy.start()

        @pl.when(has_next & (h > 0) & (h < HK - 2))
        def _():
            for copy in forward_copies(h + 2):
                copy.start()

        units = [(b, pair) for b in range(blocks) for pair in range(GROUP // 2)]

        def products(unit):
            b, pair = unit
            here = slice(b * BLK, (b + 1) * BLK)
            window = slice(b * BLK, b * BLK + span)
            heads = [h * GROUP + 2 * pair, h * GROUP + 2 * pair + 1]
            key = kw_ref[window, lanes(h, HD)]
            value = vw_ref[window, lanes(h, HD)]
            query = jnp.concatenate([q_ref[here, lanes(i, HD)] for i in heads], axis=0)
            grad = jnp.concatenate([g_ref[here, lanes(i, HD)] for i in heads], axis=0)
            scores = lax.dot_general(key, query, TRANS_B, preferred_element_type=jnp.float32)
            dprobs = lax.dot_general(value, grad, TRANS_B, preferred_element_type=jnp.float32)
            return scores, dprobs

        def softmax(unit, scores, dprobs):
            bias = bias_ref[unit[0]]
            scores = scores + jnp.concatenate([bias, bias], axis=1)
            top = jnp.max(scores, axis=0, keepdims=True)
            weights = jnp.exp2((scores - top) * EXP2_SCALE)
            inverse = 1.0 / jnp.sum(weights, axis=0, keepdims=True)
            delta = jnp.sum(weights * dprobs, axis=0, keepdims=True) * inverse
            probs = weights * inverse
            dscores = (probs * (dprobs - delta)).astype(jnp.bfloat16)
            return dscores, probs.astype(jnp.bfloat16)

        def gradients(unit, dscores, probs_low):
            b, pair = unit
            here = slice(b * BLK, (b + 1) * BLK)
            window = slice(b * BLK, b * BLK + span)
            heads = [h * GROUP + 2 * pair, h * GROUP + 2 * pair + 1]
            key = kw_ref[window, lanes(h, HD)]
            query = jnp.concatenate([q_ref[here, lanes(i, HD)] for i in heads], axis=0)
            grad = jnp.concatenate([g_ref[here, lanes(i, HD)] for i in heads], axis=0)
            grad_query = lax.dot_general(key, dscores, TRANS_A, preferred_element_type=jnp.float32)
            grad_query = jnp.transpose((grad_query * SCALE).astype(jnp.bfloat16))
            for k, i in enumerate(heads):
                gq_ref[here, lanes(i, HD)] = grad_query[k * BLK : (k + 1) * BLK]
            key_term = jnp.dot(dscores, query, preferred_element_type=jnp.float32)
            value_term = jnp.dot(probs_low, grad, preferred_element_type=jnp.float32)
            shared = slice(b * BLK, b * BLK + rows)
            fresh = slice(b * BLK + rows, b * BLK + span)
            for total, term in ((dk_ref, key_term), (dv_ref, value_term)):
                if unit == (0, 0):
                    total[h, 0:span, :] = term
                elif pair == 0:
                    total[h, shared, :] += term[:rows]
                    total[h, fresh, :] = term[rows:]
                else:
                    total[h, b * BLK : b * BLK + span, :] += term

        ready = products(units[0])
        done = None
        for at, unit in enumerate(units):
            later = products(units[at + 1]) if at + 1 < len(units) else None
            low = softmax(unit, *ready)
            if done is not None:
                gradients(*done)
            done = (unit, *low)
            ready = later
        gradients(*done)

        back_send[h, 0] = (dk_ref[h, 0:rows, :] * SCALE).astype(jnp.bfloat16)
        back_send[h, 1] = dv_ref[h, 0:rows, :].astype(jnp.bfloat16)

        @pl.when(has_prev)
        def _():
            back_copy(h).start()

        return carry

    lax.fori_loop(0, HK, head_step, 0)

    @pl.when(jnp.logical_not(has_next))
    def _():
        back_recv[...] = jnp.zeros_like(back_recv)

    for h in range(HK):

        @pl.when(has_next)
        def _():
            back_copy(h).wait_recv()

        columns = slice(h * HD, (h + 1) * HD)
        gk_ref[:, columns] = (
            dk_ref[h, rows:, :] * SCALE + back_recv[h, 0].astype(jnp.float32)
        ).astype(jnp.bfloat16)
        gv_ref[:, columns] = (
            dv_ref[h, rows:, :] + back_recv[h, 1].astype(jnp.float32)
        ).astype(jnp.bfloat16)

    @pl.when(has_next)
    def _():
        chan_copy.wait_send()
        for h in range(HK):
            for copy in forward_copies(h):
                copy.wait_send()

    @pl.when(has_prev)
    def _():
        for h in range(HK):
            back_copy(h).wait_send()


def store(gq_ref, gk_ref, gv_ref, gq_hbm, gk_hbm, gv_hbm, sem):
    copies = [
        pltpu.make_async_copy(source, target, sem.at[at])
        for at, (source, target) in enumerate(
            ((gq_ref, gq_hbm), (gk_ref, gk_hbm), (gv_ref, gv_hbm))
        )
    ]
    for copy in copies:
        copy.start()
    for copy in copies:
        copy.wait()


def per_device(queries, keys, values, grad_out, seg_starts, channels):
    rows = queries.shape[0]
    blocks = rows // BLK
    span = rows + BLK
    vmem = pl.BlockSpec(memory_space=pltpu.VMEM)
    hbm = pl.BlockSpec(memory_space=pl.ANY)
    held = pl.pallas_call(
        functools.partial(kernel, lax.axis_size("ctx")),
        out_shape=(
            pltpu.VMEM(queries.shape, jnp.bfloat16),
            pltpu.VMEM(keys.shape, jnp.bfloat16),
            pltpu.VMEM(values.shape, jnp.bfloat16),
        ),
        in_specs=[pl.BlockSpec(memory_space=pltpu.SMEM), vmem, hbm, hbm, hbm, hbm],
        out_specs=(vmem, vmem, vmem),
        scratch_shapes=[
            pltpu.VMEM((rows, HQ * HD), jnp.bfloat16),
            pltpu.VMEM((rows, HQ * HD), jnp.bfloat16),
            pltpu.VMEM((2 * rows, HK * HD), jnp.bfloat16),
            pltpu.VMEM((2 * rows, HK * HD), jnp.bfloat16),
            pltpu.VMEM((1, rows), jnp.int32),
            pltpu.VMEM((blocks, span, BLK), jnp.float32),
            pltpu.VMEM((HK, 2 * rows, HD), jnp.float32),
            pltpu.VMEM((HK, 2 * rows, HD), jnp.float32),
            pltpu.VMEM((HK, 2, rows, HD), jnp.bfloat16),
            pltpu.VMEM((HK, 2, rows, HD), jnp.bfloat16),
            pltpu.SemaphoreType.DMA((4, HK)),
            pltpu.SemaphoreType.DMA((2, HK)),
            pltpu.SemaphoreType.DMA((2, HK)),
            pltpu.SemaphoreType.DMA((2,)),
            pltpu.SemaphoreType.DMA((HK,)),
            pltpu.SemaphoreType.DMA((HK,)),
        ],
        compiler_params=pltpu.CompilerParams(
            collective_id=0, has_side_effects=True, vmem_limit_bytes=60 * 1024 * 1024
        ),
        name="window_backward",
    )(seg_starts, channels.reshape(1, rows), queries, keys, values, grad_out)
    return pl.pallas_call(
        store,
        out_shape=tuple(jax.ShapeDtypeStruct(x.shape, x.dtype) for x in (queries, keys, values)),
        in_specs=[pl.BlockSpec(memory_space=pl.ANY)] * 3,
        out_specs=(hbm,) * 3,
        scratch_shapes=[pltpu.SemaphoreType.DMA((3,))],
        compiler_params=pltpu.CompilerParams(vmem_limit_bytes=2 * 1024 * 1024),
        name="store",
    )(*held)


def solution(mesh):
    placed = (
        P(("groups", "ctx"), None),
        P(("groups", "ctx"), None),
        P(("groups", "ctx"), None),
        P(("groups", "ctx"), None),
        P("groups"),
        P(("groups", "ctx")),
    )
    return jax.shard_map(
        per_device,
        mesh=mesh,
        in_specs=placed,
        out_specs=(
            P(("groups", "ctx"), None),
            P(("groups", "ctx"), None),
            P(("groups", "ctx"), None),
        ),
        check_vma=False,
    )
```
